32 devices in a mesh: row: 8 (over z, y), col: 4 (over x, core).
Axes of the slice: x: 2, y: 2, z: 4, core: 2. Of those that a mesh axis runs over, the one named last changes fastest.
Arguments:
- amplitudes: bfloat16 [4096, 16384], P(('row', 'col')), may hold values from -6 to 6
- amp_tiles: int32 [64, 256], P(('row', 'col')), may hold values 0 or 1
- integrals: bfloat16 [512, 16384], P('row', 'col'), may hold values from -0.046875 to 0.046875
- int_tiles: int32 [8, 256], P(None, 'col'), may hold values 0 or 1
Outputs:
- ladder: bfloat16 [512, 4096], P('col', 'row')
The draws below stay inside these ranges and needn't reach their ends.
All inputs are finite; a program needn't handle non-finite values. No bound on the sum of `amp_tiles` or of `int_tiles` on one device may be relied on, other than what follows from the above.
Results may differ from the reference program's by a relative error of at most 0.001.
Values may be sent and summed in bfloat16 or wider, within the bound.
A program may use at most 64 MiB of HBM per device.

```python
import jax
import jax.numpy as jnp
from jax import lax

TILE = 64
K = 16384
A = 512
P_SIZE = 4096
N_ROW = 8


def set_ends(values, own_key, least, largest):
    extent = values.shape
    place = [jax.random.randint(jax.random.fold_in(own_key, axis), (), 0, extent[axis]) for axis in range(len(extent))]
    values = values.at[tuple(place)].set(least)
    longest = extent.index(max(extent))
    place[longest] = (place[longest] + 1) % extent[longest]
    return values.at[tuple(place)].set(largest)


def shard_levels(key, shape, shards, least, largest):
    loudness = 1.0
    for position, parts in shards:
        steps = jax.random.uniform(jax.random.fold_in(jax.random.fold_in(key, 6), position), (parts,), jnp.float32, least / len(shards), largest / len(shards))
        loudness = loudness * jnp.repeat(jnp.exp(steps), shape[position] // parts).reshape((-1,) + (1,) * (len(shape) - 1 - position))
    return loudness


def bell_draw(stream_key, extent, spread, most, cuts=(), kind=jnp.bfloat16):
    array = spread * jax.random.normal(stream_key, extent, jnp.float32)
    if cuts:
        array = array * shard_levels(stream_key, extent, cuts, -0.22, 0.18)
    return jnp.clip(array, -most, most).astype(kind)


def setup_inputs(seed: int = 0) -> dict:
    keys = jax.random.split(jax.random.key(seed), 5)
    return {
        "amplitudes": bell_draw(keys[0], (P_SIZE, K), 1.0, 6.0, ((0, 32),)),
        "amp_tiles": set_ends((jax.random.randint(keys[1], (P_SIZE // TILE, K // TILE), 0, 4) < 3).astype(jnp.int32), jax.random.fold_in(keys[1], 1), 0, 1),
        "integrals": bell_draw(keys[2], (A, K), K ** -0.5, 0.046875, ((0, 8), (1, 4))),
        "int_tiles": set_ends((jax.random.randint(keys[3], (A // TILE, K // TILE), 0, 4) < 3).astype(jnp.int32), jax.random.fold_in(keys[3], 1), 0, 1),
    }


def expand_mask(tiles):
    return jnp.repeat(jnp.repeat(tiles, TILE, axis=0), TILE, axis=1).astype(jnp.bfloat16)


def reference(amplitudes, amp_tiles, integrals, int_tiles):
    stored_ints = integrals * expand_mask(int_tiles)
    amp_blocks = amplitudes.reshape(N_ROW, P_SIZE // N_ROW, K)
    tile_blocks = amp_tiles.reshape(N_ROW, P_SIZE // N_ROW // TILE, K // TILE)

    def block_ladder(operands):
        amplitude_block, tile_block = operands
        stored_amps = amplitude_block * expand_mask(tile_block)
        result = lax.dot_general(stored_ints, stored_amps, (((1,), (1,)), ((), ())), preferred_element_type=jnp.float32)
        return result.astype(jnp.bfloat16)

    blocks = lax.map(block_ladder, (amp_blocks, tile_blocks))
    return jnp.transpose(blocks, (1, 0, 2)).reshape(A, P_SIZE)
```

```python
import functools

import jax
import jax.numpy as jnp
from jax import lax
from jax.experimental import pallas as pl
from jax.experimental.pallas import tpu as pltpu
from jax.sharding import PartitionSpec as P

TILE = 64
LANES = 128
CHUNKS = 4
MESH = pl.DeviceIdType.MESH


def kernel(
    n_row, n_col, amp_ref, amp_tiles, int_ref, int_tiles, out_ref,
    raw, amps, ints_raw, ints, part, pair_in, chip_in,
    load_sem, int_load_sem, amp_send, amp_recv, ring_send, ring_recv, pair_send, pair_recv, chip_send, chip_recv,
):
    row, col = lax.axis_index("row"), lax.axis_index("col")
    n_chip = n_col // 2
    chip, core = col // 2, lax.rem(col, 2)
    n_pairs = amp_ref.shape[0]
    own_rows, depth = int_ref.shape
    width = depth // CHUNKS
    n_res = ints.shape[0]
    out_rows = n_res // n_col
    half = depth // 2

    def peer(chip_step, core_step):
        return lax.rem(chip + chip_step, n_chip) * 2 + lax.rem(core + core_step, 2)

    def at_position(position):
        position = lax.rem(position + n_row, n_row)
        return jnp.where(position < n_row // 2, 2 * position, 2 * (n_row - 1 - position) + 1)

    position = jnp.where(lax.rem(row, 2) == 0, row // 2, n_row - 1 - row // 2)
    right, left = at_position(position + 1), at_position(position - 1)

    order = [(chip_step, core_step) for chip_step in range(1, n_chip) for core_step in range(2)] + [(0, 1), (0, 0)]

    def slot_of(chip_step, core_step, chunk):
        return (chip_step * 2 + core_step) * CHUNKS + chunk

    int_load = pltpu.make_async_copy(int_ref, ints_raw, int_load_sem)
    int_load.start()
    loads = {}
    for chip_step, core_step in order:
        target = peer(chip_step, core_step)
        for chunk in range(CHUNKS):
            slot = slot_of(chip_step, core_step, chunk)
            start = pl.multiple_of(target * depth + chunk * width, LANES)
            loads[slot] = pltpu.make_async_copy(amp_ref.at[:, pl.ds(start, width)], raw.at[slot], load_sem.at[slot])
            loads[slot].start()

    barrier = pltpu.get_barrier_semaphore()
    for neighbour in (left, right):
        pl.semaphore_signal(barrier, inc=1, device_id={"row": neighbour}, device_id_type=MESH)
    for chip_step, core_step in order[:-1]:
        pl.semaphore_signal(barrier, inc=1, device_id={"col": peer(chip_step, core_step)}, device_id_type=MESH)

    first_half = lax.broadcasted_iota(jnp.int32, (16, LANES), 1) < TILE

    int_load.wait()
    own_start = pl.multiple_of(row * own_rows, 16)

    def mask_ints(block, _):
        lanes = pl.ds(pl.multiple_of(block * LANES, LANES), LANES)
        for group in range(own_rows // 16):
            tile_row = (own_start + group * 16) // TILE
            mask = jnp.where(first_half, int_tiles[tile_row, 2 * block], int_tiles[tile_row, 2 * block + 1])
            mask = mask.astype(jnp.float32).astype(jnp.bfloat16)
            ints[pl.ds(own_start + group * 16, 16), lanes] = ints_raw[pl.ds(group * 16, 16), lanes] * mask
        return 0

    lax.fori_loop(0, depth // LANES, mask_ints, 0)

    pl.semaphore_wait(barrier, 2 + n_col - 1)

    limits = ((n_row // 2, n_row - 1 - n_row // 2), (n_row - 1 - n_row // 2, n_row // 2))

    def ring_copy(direction, step, part_index):
        sign = 1 if direction == 0 else -1
        origin = at_position(position - sign * (step - 1))
        block = ints.at[pl.ds(pl.multiple_of(origin * own_rows, 16), own_rows), pl.ds(part_index * half, half)]
        return pltpu.make_async_remote_copy(
            src_ref=block, dst_ref=block,
            send_sem=ring_send.at[direction, step - 1, part_index],
            recv_sem=ring_recv.at[direction, step - 1, part_index],
            device_id={"row": right if direction == 0 else left}, device_id_type=MESH,
        )

    def ring_moves(step):
        return [(d, h) for h in range(2) for d in range(2) if step <= limits[d][h]]

    for direction, part_index in ring_moves(1):
        ring_copy(direction, 1, part_index).start()

    def masked_amps(slot, target, chunk, write):
        for tile_row in range(n_pairs // TILE):
            for block in range(width // LANES):
                tile = target * (depth // TILE) + chunk * (width // TILE) + 2 * block
                mask = jnp.where(first_half, amp_tiles[tile_row, tile], amp_tiles[tile_row, tile + 1])
                mask = mask.astype(jnp.float32).astype(jnp.bfloat16)
                for group in range(TILE // 16):
                    rows = pl.ds(tile_row * TILE + group * 16, 16)
                    write(tile_row * TILE + group * 16, block, raw[slot, rows, pl.ds(block * LANES, LANES)] * mask)

    def amp_copy(chip_step, core_step, chunk):
        slot = slot_of(chip_step, core_step, chunk)
        return pltpu.make_async_remote_copy(
            src_ref=raw.at[slot],
            dst_ref=amps.at[pl.ds(pl.multiple_of(col * n_pairs, 16), n_pairs), pl.ds(chunk * width, width)],
            send_sem=amp_send.at[slot], recv_sem=amp_recv.at[slot],
            device_id={"col": peer(chip_step, core_step)}, device_id_type=MESH,
        )

    sends = [(s, c, q) for q in range(CHUNKS) for s, c in order[:-2]] + [(0, 1, q) for q in range(CHUNKS)]
    for chip_step, core_step, chunk in sends:
        slot = slot_of(chip_step, core_step, chunk)
        loads[slot].wait()

        def write(row_start, block, value):
            raw[slot, pl.ds(row_start, 16), pl.ds(block * LANES, LANES)] = value

        masked_amps(slot, peer(chip_step, core_step), chunk, write)
        amp_copy(chip_step, core_step, chunk).start()
    own_pairs = pl.multiple_of(col * n_pairs, 16)
    for chunk in range(CHUNKS):
        slot = slot_of(0, 0, chunk)
        loads[slot].wait()

        def write(row_start, block, value):
            amps[pl.ds(own_pairs + row_start, 16), pl.ds(chunk * width + block * LANES, LANES)] = value

        masked_amps(slot, col, chunk, write)

    for step in range(1, n_row // 2 + 1):
        for direction, part_index in ring_moves(step):
            ring_copy(direction, step, part_index).wait_recv()
            if step + 1 <= limits[direction][part_index]:
                ring_copy(direction, step + 1, part_index).start()

    m_tile = 256

    def multiply(chip_step, chunk, first):
        source = lax.rem(chip - chip_step + n_chip, n_chip)
        pairs = pl.ds(pl.multiple_of(source * (2 * n_pairs), LANES), 2 * n_pairs)
        lanes = pl.ds(chunk * width, width)

        def body(tile, _):
            rows = pl.ds(pl.multiple_of(tile * m_tile, m_tile), m_tile)
            product = lax.dot_general(
                ints[rows, lanes], amps[pairs, lanes], (((1,), (1,)), ((), ())), preferred_element_type=jnp.float32
            )
            part[rows, pairs] = product if first else part[rows, pairs] + product
            return 0

        lax.fori_loop(0, n_res // m_tile, body, 0)

    for chunk in range(CHUNKS):
        amp_copy(0, 1, chunk).wait_recv()
        multiply(0, chunk, chunk == 0)
    for chunk in range(CHUNKS):
        for chip_step in range(1, n_chip):
            for core_step in range(2):
                amp_copy(chip_step, core_step, chunk).wait_recv()
            multiply(chip_step, chunk, chunk == 0)

    def res_rows(chip_step, core_step):
        return pl.ds(pl.multiple_of(peer(chip_step, core_step) * out_rows, 8), out_rows)

    def pair_copy(chip_step):
        return pltpu.make_async_remote_copy(
            src_ref=part.at[res_rows(chip_step, 1)], dst_ref=pair_in.at[chip_step],
            send_sem=pair_send.at[chip_step], recv_sem=pair_recv.at[chip_step],
            device_id={"col": peer(0, 1)}, device_id_type=MESH,
        )

    def chip_copy(chip_step):
        return pltpu.make_async_remote_copy(
            src_ref=part.at[res_rows(chip_step, 0)], dst_ref=chip_in.at[chip_step - 1],
            send_sem=chip_send.at[chip_step - 1], recv_sem=chip_recv.at[chip_step - 1],
            device_id={"col": peer(chip_step, 0)}, device_id_type=MESH,
        )

    steps = list(range(1, n_chip)) + [0]
    for chip_step in steps:
        pair_copy(chip_step).start()
    for chip_step in steps:
        pair_copy(chip_step).wait_recv()
        rows = res_rows(chip_step, 0)
        part[rows, :] = part[rows, :] + pair_in[chip_step]
        if chip_step:
            chip_copy(chip_step).start()
    total = part[res_rows(0, 0), :]
    for chip_step in range(1, n_chip):
        chip_copy(chip_step).wait_recv()
        total = total + chip_in[chip_step - 1]
    out_ref[...] = total.astype(out_ref.dtype)

    for chip_step, core_step, chunk in sends:
        amp_copy(chip_step, core_step, chunk).wait_send()
    for step in range(1, n_row // 2 + 1):
        for direction, part_index in ring_moves(step):
            ring_copy(direction, step, part_index).wait_send()
    for chip_step in steps:
        pair_copy(chip_step).wait_send()
        if chip_step:
            chip_copy(chip_step).wait_send()


def local(n_row, n_col, amplitudes, amp_tiles, integrals, int_tiles):
    n_pairs = amplitudes.shape[0]
    own_rows, depth = integrals.shape
    n_res, row_pairs = own_rows * n_row, n_pairs * n_col
    out_rows, n_chip = n_res // n_col, n_col // 2
    slots = n_col * CHUNKS
    return pl.pallas_call(
        functools.partial(kernel, n_row, n_col),
        out_shape=jax.ShapeDtypeStruct((out_rows, row_pairs), jnp.bfloat16),
        in_specs=[
            pl.BlockSpec(memory_space=pl.ANY),
            pl.BlockSpec(memory_space=pltpu.SMEM),
            pl.BlockSpec(memory_space=pl.ANY),
            pl.BlockSpec(memory_space=pltpu.SMEM),
        ],
        out_specs=pl.BlockSpec(memory_space=pltpu.VMEM),
        scratch_shapes=[
            pltpu.VMEM((slots, n_pairs, depth // CHUNKS), jnp.bfloat16),
            pltpu.VMEM((row_pairs, depth), jnp.bfloat16),
            pltpu.VMEM((own_rows, depth), jnp.bfloat16),
            pltpu.VMEM((n_res, depth), jnp.bfloat16),
            pltpu.VMEM((n_res, row_pairs), jnp.float32),
            pltpu.VMEM((n_chip, out_rows, row_pairs), jnp.float32),
            pltpu.VMEM((n_chip - 1, out_rows, row_pairs), jnp.float32),
            pltpu.SemaphoreType.DMA((slots,)),
            pltpu.SemaphoreType.DMA,
            pltpu.SemaphoreType.DMA((slots,)),
            pltpu.SemaphoreType.DMA((slots,)),
            pltpu.SemaphoreType.DMA((2, n_row // 2, 2)),
            pltpu.SemaphoreType.DMA((2, n_row // 2, 2)),
            pltpu.SemaphoreType.DMA((n_chip,)),
            pltpu.SemaphoreType.DMA((n_chip,)),
            pltpu.SemaphoreType.DMA((n_chip - 1,)),
            pltpu.SemaphoreType.DMA((n_chip - 1,)),
        ],
        compiler_params=pltpu.CompilerParams(
            collective_id=0, has_side_effects=True, vmem_limit_bytes=48 * 1024 * 1024
        ),
    )(amplitudes, amp_tiles, integrals, int_tiles)


def solution(mesh):
    return jax.shard_map(
        functools.partial(local, mesh.shape["row"], mesh.shape["col"]),
        mesh=mesh,
        in_specs=(
            P(("row", "col"), None),
            P(("row", "col"), None),
            P("row", "col"),
            P(None, "col"),
        ),
        out_specs=P("col", "row"),
        check_vma=False,
    )
```

```python
import functools

import jax
import jax.numpy as jnp
from jax import lax
from jax.experimental import pallas as pl
from jax.experimental.pallas import tpu as pltpu
from jax.sharding import PartitionSpec as P

TILE = 64
LANES = 128
CHUNKS = 4
MESH = pl.DeviceIdType.MESH


def kernel(
    n_row, n_col, amp_ref, amp_tiles_ref, int_ref, int_tiles_ref, out_ref,
    amp_tiles, int_tiles, tile_sem, raw, amps, ints_raw, ints, part, pair_in, chip_in,
    load_sem, int_load_sem, amp_send, amp_recv, ring_send, ring_recv, pair_send, pair_recv, chip_send, chip_recv,
):
    row, col = lax.axis_index("row"), lax.axis_index("col")
    n_chip = n_col // 2
    chip, core = col // 2, lax.rem(col, 2)
    n_pairs = amp_ref.shape[0]
    own_rows, depth = int_ref.shape
    width = depth // CHUNKS
    n_res = ints.shape[0]
    out_rows = n_res // n_col
    half = depth // 2

    def peer(chip_step, core_step):
        return lax.rem(chip + chip_step, n_chip) * 2 + lax.rem(core + core_step, 2)

    def at_position(position):
        position = lax.rem(position + n_row, n_row)
        return jnp.where(position < n_row // 2, 2 * position, 2 * (n_row - 1 - position) + 1)

    position = jnp.where(lax.rem(row, 2) == 0, row // 2, n_row - 1 - row // 2)
    right, left = at_position(position + 1), at_position(position - 1)

    order = [(chip_step, core_step) for chip_step in range(1, n_chip) for core_step in range(2)] + [(0, 1), (0, 0)]

    barrier = pltpu.get_barrier_semaphore()
    for neighbour in (left, right):
        pl.semaphore_signal(barrier, inc=1, device_id={"row": neighbour}, device_id_type=MESH)
    for chip_step, core_step in order[:-1]:
        pl.semaphore_signal(barrier, inc=1, device_id={"col": peer(chip_step, core_step)}, device_id_type=MESH)

    def slot_of(chip_step, core_step, chunk):
        return (chip_step * 2 + core_step) * CHUNKS + chunk

    sends = [(s, c, q) for q in range(CHUNKS) for s, c in order[:-2]] + [(0, 1, q) for q in range(CHUNKS)]

    int_load = pltpu.make_async_copy(int_ref, ints_raw, int_load_sem)
    tile_loads = [
        pltpu.make_async_copy(amp_tiles_ref, amp_tiles, tile_sem.at[0]),
        pltpu.make_async_copy(int_tiles_ref, int_tiles, tile_sem.at[1]),
    ]
    for load in tile_loads:
        load.start()
    loads = {}
    for chip_step, core_step in order:
        target = peer(chip_step, core_step)
        for chunk in range(CHUNKS):
            slot = slot_of(chip_step, core_step, chunk)
            start = pl.multiple_of(target * depth + chunk * width, LANES)
            loads[slot] = pltpu.make_async_copy(amp_ref.at[:, pl.ds(start, width)], raw.at[slot], load_sem.at[slot])
    for index, (chip_step, core_step, chunk) in enumerate(sends + [(0, 0, q) for q in range(CHUNKS)]):
        loads[slot_of(chip_step, core_step, chunk)].start()
        if index == 0:
            int_load.start()

    first_half = lax.broadcasted_iota(jnp.int32, (16, LANES), 1) < TILE

    def masked_amps(slot, target, chunk, write):
        for tile_row in range(n_pairs // TILE):
            for block in range(width // LANES):
                tile = target * (depth // TILE) + chunk * (width // TILE) + 2 * block
                mask = jnp.where(first_half, amp_tiles[tile_row, tile], amp_tiles[tile_row, tile + 1])
                mask = mask.astype(jnp.float32).astype(jnp.bfloat16)
                for group in range(TILE // 16):
                    rows = pl.ds(tile_row * TILE + group * 16, 16)
                    write(tile_row * TILE + group * 16, block, raw[slot, rows, pl.ds(block * LANES, LANES)] * mask)

    def amp_copy(chip_step, core_step, chunk):
        slot = slot_of(chip_step, core_step, chunk)
        return pltpu.make_async_remote_copy(
            src_ref=raw.at[slot],
            dst_ref=amps.at[pl.ds(pl.multiple_of(col * n_pairs, 16), n_pairs), pl.ds(chunk * width, width)],
            send_sem=amp_send.at[slot], recv_sem=amp_recv.at[slot],
            device_id={"col": peer(chip_step, core_step)}, device_id_type=MESH,
        )

    def prepare_amps(chip_step, core_step, chunk):
        slot = slot_of(chip_step, core_step, chunk)
        loads[slot].wait()

        def write(row_start, block, value):
            raw[slot, pl.ds(row_start, 16), pl.ds(block * LANES, LANES)] = value

        masked_amps(slot, peer(chip_step, core_step), chunk, write)
    tile_loads[0].wait()
    prepare_amps(*sends[0])
    pl.semaphore_wait(barrier, 2 + n_col - 1)
    amp_copy(*sends[0]).start()

    int_load.wait()
    tile_loads[1].wait()
    own_start = pl.multiple_of(row * own_rows, 16)

    def mask_ints(block, _):
        lanes = pl.ds(pl.multiple_of(block * LANES, LANES), LANES)
        for group in range(own_rows // 16):
            tile_row = (own_start + group * 16) // TILE
            mask = jnp.where(first_half, int_tiles[tile_row, 2 * block], int_tiles[tile_row, 2 * block + 1])
            mask = mask.astype(jnp.float32).astype(jnp.bfloat16)
            ints[pl.ds(own_start + group * 16, 16), lanes] = ints_raw[pl.ds(group * 16, 16), lanes] * mask
        return 0

    lax.fori_loop(0, depth // LANES, mask_ints, 0)

    limits = ((n_row // 2, n_row - 1 - n_row // 2), (n_row - 1 - n_row // 2, n_row // 2))

    def ring_copy(direction, step, part_index):
        sign = 1 if direction == 0 else -1
        origin = at_position(position - sign * (step - 1))
        block = ints.at[pl.ds(pl.multiple_of(origin * own_rows, 16), own_rows), pl.ds(part_index * half, half)]
        return pltpu.make_async_remote_copy(
            src_ref=block, dst_ref=block,
            send_sem=ring_send.at[direction, step - 1, part_index],
            recv_sem=ring_recv.at[direction, step - 1, part_index],
            device_id={"row": right if direction == 0 else left}, device_id_type=MESH,
        )

    def ring_moves(step):
        return [(d, h) for h in range(2) for d in range(2) if step <= limits[d][h]]

    for direction, part_index in ring_moves(1):
        ring_copy(direction, 1, part_index).start()

    for send in sends[1:]:
        prepare_amps(*send)
        amp_copy(*send).start()

    own_pairs = pl.multiple_of(col * n_pairs, 16)
    for chunk in range(CHUNKS):
        slot = slot_of(0, 0, chunk)
        loads[slot].wait()

        def write(row_start, block, value):
            amps[pl.ds(own_pairs + row_start, 16), pl.ds(chunk * width + block * LANES, LANES)] = value

        masked_amps(slot, col, chunk, write)

    for step in range(1, n_row // 2 + 1):
        for direction, part_index in ring_moves(step):
            ring_copy(direction, step, part_index).wait_recv()
            if step + 1 <= limits[direction][part_index]:
                ring_copy(direction, step + 1, part_index).start()

    m_tile = 256

    def multiply(chip_step, chunk, first):
        pairs = group_pairs(chip_step)
        lanes = pl.ds(chunk * width, width)

        def body(tile, _):
            rows = pl.ds(pl.multiple_of(tile * m_tile, m_tile), m_tile)
            product = lax.dot_general(
                ints[rows, lanes], amps[pairs, lanes], (((1,), (1,)), ((), ())), preferred_element_type=jnp.float32
            )
            part[rows, pairs] = product if first else part[rows, pairs] + product
            return 0

        lax.fori_loop(0, n_res // m_tile, body, 0)

    def res_rows(chip_step, core_step):
        return pl.ds(pl.multiple_of(peer(chip_step, core_step) * out_rows, 8), out_rows)

    def group_pairs(group):
        source = lax.rem(chip - group + n_chip, n_chip)
        return pl.ds(pl.multiple_of(source * (2 * n_pairs), LANES), 2 * n_pairs)

    def pair_copy(group, chip_step):
        pairs = group_pairs(group)
        return pltpu.make_async_remote_copy(
            src_ref=part.at[res_rows(chip_step, 1), pairs], dst_ref=pair_in.at[chip_step, :, pairs],
            send_sem=pair_send.at[group, chip_step], recv_sem=pair_recv.at[group, chip_step],
            device_id={"col": peer(0, 1)}, device_id_type=MESH,
        )

    def chip_copy(group, chip_step):
        pairs = group_pairs(group)
        return pltpu.make_async_remote_copy(
            src_ref=part.at[res_rows(chip_step, 0), pairs], dst_ref=chip_in.at[chip_step - 1, :, pairs],
            send_sem=chip_send.at[group, chip_step - 1], recv_sem=chip_recv.at[group, chip_step - 1],
            device_id={"col": peer(chip_step, 0)}, device_id_type=MESH,
        )

    def chip_arrival(group, chip_step):
        pairs = group_pairs(group)
        sender_group = (group - chip_step) % n_chip
        return pltpu.make_async_remote_copy(
            src_ref=part.at[res_rows(chip_step, 0), pairs], dst_ref=chip_in.at[chip_step - 1, :, pairs],
            send_sem=chip_send.at[sender_group, chip_step - 1], recv_sem=chip_recv.at[sender_group, chip_step - 1],
            device_id={"col": peer(chip_step, 0)}, device_id_type=MESH,
        )

    steps = list(range(1, n_chip)) + [0]

    def exchange(group):
        for chip_step in steps:
            pair_copy(group, chip_step).start()

    def pass_on(group):
        pairs = group_pairs(group)
        for chip_step in steps:
            pair_copy(group, chip_step).wait_recv()
            rows = res_rows(chip_step, 0)
            part[rows, pairs] = part[rows, pairs] + pair_in[chip_step, :, pairs]
            if chip_step:
                chip_copy(group, chip_step).start()

    for chunk in range(CHUNKS):
        amp_copy(0, 1, chunk).wait_recv()
        multiply(0, chunk, chunk == 0)
    exchange(0)
    for group in range(1, n_chip):
        for chunk in range(CHUNKS):
            for core_step in range(2):
                amp_copy(group, core_step, chunk).wait_recv()
            multiply(group, chunk, chunk == 0)
            if group == 1 and chunk == 0:
                pass_on(0)
        exchange(group)
    for group in range(1, n_chip):
        pass_on(group)
    for group in range(n_chip):
        pairs = group_pairs(group)
        total = part[res_rows(0, 0), pairs]
        for chip_step in range(1, n_chip):
            chip_arrival(group, chip_step).wait_recv()
            total = total + chip_in[chip_step - 1, :, pairs]
        out_ref[:, pairs] = total.astype(out_ref.dtype)

    for chip_step, core_step, chunk in sends:
        amp_copy(chip_step, core_step, chunk).wait_send()
    for step in range(1, n_row // 2 + 1):
        for direction, part_index in ring_moves(step):
            ring_copy(direction, step, part_index).wait_send()
    for group in range(n_chip):
        for chip_step in steps:
            pair_copy(group, chip_step).wait_send()
            if chip_step:
                chip_copy(group, chip_step).wait_send()


def local(n_row, n_col, amplitudes, amp_tiles, integrals, int_tiles):
    n_pairs = amplitudes.shape[0]
    own_rows, depth = integrals.shape
    n_res, row_pairs = own_rows * n_row, n_pairs * n_col
    out_rows, n_chip = n_res // n_col, n_col // 2
    slots = n_col * CHUNKS
    return pl.pallas_call(
        functools.partial(kernel, n_row, n_col),
        out_shape=jax.ShapeDtypeStruct((out_rows, row_pairs), jnp.bfloat16),
        in_specs=[
            pl.BlockSpec(memory_space=pltpu.HBM),
            pl.BlockSpec(memory_space=pltpu.HBM),
            pl.BlockSpec(memory_space=pltpu.HBM),
            pl.BlockSpec(memory_space=pltpu.HBM),
        ],
        out_specs=pl.BlockSpec(memory_space=pltpu.VMEM),
        scratch_shapes=[
            pltpu.SMEM(amp_tiles.shape, jnp.int32),
            pltpu.SMEM(int_tiles.shape, jnp.int32),
            pltpu.SemaphoreType.DMA((2,)),
            pltpu.VMEM((slots, n_pairs, depth // CHUNKS), jnp.bfloat16),
            pltpu.VMEM((row_pairs, depth), jnp.bfloat16),
            pltpu.VMEM((own_rows, depth), jnp.bfloat16),
            pltpu.VMEM((n_res, depth), jnp.bfloat16),
            pltpu.VMEM((n_res, row_pairs), jnp.float32),
            pltpu.VMEM((n_chip, out_rows, row_pairs), jnp.float32),
            pltpu.VMEM((n_chip - 1, out_rows, row_pairs), jnp.float32),
            pltpu.SemaphoreType.DMA((slots,)),
            pltpu.SemaphoreType.DMA,
            pltpu.SemaphoreType.DMA((slots,)),
            pltpu.SemaphoreType.DMA((slots,)),
            pltpu.SemaphoreType.DMA((2, n_row // 2, 2)),
            pltpu.SemaphoreType.DMA((2, n_row // 2, 2)),
            pltpu.SemaphoreType.DMA((n_chip, n_chip)),
            pltpu.SemaphoreType.DMA((n_chip, n_chip)),
            pltpu.SemaphoreType.DMA((n_chip, n_chip - 1)),
            pltpu.SemaphoreType.DMA((n_chip, n_chip - 1)),
        ],
        compiler_params=pltpu.CompilerParams(
            collective_id=0, has_side_effects=True, vmem_limit_bytes=64 * 1024 * 1024
        ),
    )(amplitudes, amp_tiles, integrals, int_tiles)


def solution(mesh):
    return jax.shard_map(
        functools.partial(local, mesh.shape["row"], mesh.shape["col"]),
        mesh=mesh,
        in_specs=(
            P(("row", "col"), None),
            P(("row", "col"), None),
            P("row", "col"),
            P(None, "col"),
        ),
        out_specs=P("col", "row"),
        check_vma=False,
    )
```

```python
import functools

import jax
import jax.numpy as jnp
from jax import lax
from jax.experimental import pallas as pl
from jax.experimental.pallas import tpu as pltpu
from jax.sharding import PartitionSpec as P

TILE = 64
LANES = 128
CHUNKS = 2
MESH = pl.DeviceIdType.MESH


def kernel(
    n_row, n_col, amp_ref, amp_tiles_ref, int_ref, int_tiles_ref, out_ref,
    amp_tiles, int_tiles, tile_sem, raw, amps, ints_raw, ints, part, pair_in, chip_in,
    load_sem, int_load_sem, amp_send, amp_recv, ring_send, ring_recv, pair_send, pair_recv, chip_send, chip_recv,
):
    row, col = lax.axis_index("row"), lax.axis_index("col")
    n_chip = n_col // 2
    chip, core = col // 2, lax.rem(col, 2)
    n_pairs = amp_ref.shape[0]
    own_rows, depth = int_ref.shape
    width = depth // CHUNKS
    n_res = ints.shape[0]
    out_rows = n_res // n_col
    half = depth // 2

    def peer(chip_step, core_step):
        return lax.rem(chip + chip_step, n_chip) * 2 + lax.rem(core + core_step, 2)

    def at_position(position):
        position = lax.rem(position + n_row, n_row)
        return jnp.where(position < n_row // 2, 2 * position, 2 * (n_row - 1 - position) + 1)

    position = jnp.where(lax.rem(row, 2) == 0, row // 2, n_row - 1 - row // 2)
    right, left = at_position(position + 1), at_position(position - 1)

    order = [(chip_step, core_step) for chip_step in range(1, n_chip) for core_step in range(2)] + [(0, 1), (0, 0)]

    barrier = pltpu.get_barrier_semaphore()
    for neighbour in (left, right):
        pl.semaphore_signal(barrier, inc=1, device_id={"row": neighbour}, device_id_type=MESH)
    for chip_step, core_step in order[:-1]:
        pl.semaphore_signal(barrier, inc=1, device_id={"col": peer(chip_step, core_step)}, device_id_type=MESH)

    def slot_of(chip_step, core_step, chunk):
        return (chip_step * 2 + core_step) * CHUNKS + chunk

    across = [(s, c, q) for q in range(CHUNKS) for s, c in order[:-2]]
    sends = across[:2] + [(0, 1, q) for q in range(CHUNKS)] + across[2:]

    int_load = pltpu.make_async_copy(int_ref, ints_raw, int_load_sem)
    tile_loads = [
        pltpu.make_async_copy(amp_tiles_ref, amp_tiles, tile_sem.at[0]),
        pltpu.make_async_copy(int_tiles_ref, int_tiles, tile_sem.at[1]),
    ]
    for load in tile_loads:
        load.start()
    loads = {}
    for chip_step, core_step in order:
        target = peer(chip_step, core_step)
        for chunk in range(CHUNKS):
            slot = slot_of(chip_step, core_step, chunk)
            start = pl.multiple_of(target * depth + chunk * width, LANES)
            loads[slot] = pltpu.make_async_copy(amp_ref.at[:, pl.ds(start, width)], raw.at[slot], load_sem.at[slot])
    for index, (chip_step, core_step, chunk) in enumerate(sends + [(0, 0, q) for q in range(CHUNKS)]):
        loads[slot_of(chip_step, core_step, chunk)].start()
        if index == 0:
            int_load.start()

    first_half = lax.broadcasted_iota(jnp.int32, (16, LANES), 1) < TILE

    def masked_amps(slot, target, chunk, write):
        for tile_row in range(n_pairs // TILE):
            for block in range(width // LANES):
                tile = target * (depth // TILE) + chunk * (width // TILE) + 2 * block
                mask = jnp.where(first_half, amp_tiles[tile_row, tile], amp_tiles[tile_row, tile + 1])
                mask = mask.astype(jnp.float32).astype(jnp.bfloat16)
                for group in range(TILE // 16):
                    rows = pl.ds(tile_row * TILE + group * 16, 16)
                    write(tile_row * TILE + group * 16, block, raw[slot, rows, pl.ds(block * LANES, LANES)] * mask)

    def amp_copy(chip_step, core_step, chunk):
        slot = slot_of(chip_step, core_step, chunk)
        return pltpu.make_async_remote_copy(
            src_ref=raw.at[slot],
            dst_ref=amps.at[pl.ds(pl.multiple_of(col * n_pairs, 16), n_pairs), pl.ds(chunk * width, width)],
            send_sem=amp_send.at[slot], recv_sem=amp_recv.at[slot],
            device_id={"col": peer(chip_step, core_step)}, device_id_type=MESH,
        )

    def prepare_amps(chip_step, core_step, chunk):
        slot = slot_of(chip_step, core_step, chunk)
        loads[slot].wait()

        def write(row_start, block, value):
            raw[slot, pl.ds(row_start, 16), pl.ds(block * LANES, LANES)] = value

        masked_amps(slot, peer(chip_step, core_step), chunk, write)
    tile_loads[0].wait()
    prepare_amps(*sends[0])
    pl.semaphore_wait(barrier, 2 + n_col - 1)
    amp_copy(*sends[0]).start()

    int_load.wait()
    tile_loads[1].wait()
    own_start = pl.multiple_of(row * own_rows, 16)

    def mask_ints(block, _):
        lanes = pl.ds(pl.multiple_of(block * LANES, LANES), LANES)
        for group in range(own_rows // 16):
            tile_row = (own_start + group * 16) // TILE
            mask = jnp.where(first_half, int_tiles[tile_row, 2 * block], int_tiles[tile_row, 2 * block + 1])
            mask = mask.astype(jnp.float32).astype(jnp.bfloat16)
            ints[pl.ds(own_start + group * 16, 16), lanes] = ints_raw[pl.ds(group * 16, 16), lanes] * mask
        return 0

    lax.fori_loop(0, depth // LANES, mask_ints, 0)

    limits = ((n_row // 2, n_row - 1 - n_row // 2), (n_row - 1 - n_row // 2, n_row // 2))

    def ring_copy(direction, step, part_index):
        sign = 1 if direction == 0 else -1
        origin = at_position(position - sign * (step - 1))
        block = ints.at[pl.ds(pl.multiple_of(origin * own_rows, 16), own_rows), pl.ds(part_index * half, half)]
        return pltpu.make_async_remote_copy(
            src_ref=block, dst_ref=block,
            send_sem=ring_send.at[direction, step - 1, part_index],
            recv_sem=ring_recv.at[direction, step - 1, part_index],
            device_id={"row": right if direction == 0 else left}, device_id_type=MESH,
        )

    def ring_moves(step):
        return [(d, h) for h in range(2) for d in range(2) if step <= limits[d][h]]

    for direction, part_index in ring_moves(1):
        ring_copy(direction, 1, part_index).start()

    for send in sends[1:]:
        prepare_amps(*send)
        amp_copy(*send).start()

    own_pairs = pl.multiple_of(col * n_pairs, 16)
    for chunk in range(CHUNKS):
        slot = slot_of(0, 0, chunk)
        loads[slot].wait()

        def write(row_start, block, value):
            amps[pl.ds(own_pairs + row_start, 16), pl.ds(chunk * width + block * LANES, LANES)] = value

        masked_amps(slot, col, chunk, write)

    for step in range(1, n_row // 2 + 1):
        for direction, part_index in ring_moves(step):
            ring_copy(direction, step, part_index).wait_recv()
            if step + 1 <= limits[direction][part_index]:
                ring_copy(direction, step + 1, part_index).start()

    m_tile = 256

    def multiply(chip_step, chunk, first):
        source = lax.rem(chip - chip_step + n_chip, n_chip)
        pairs = pl.ds(pl.multiple_of(source * (2 * n_pairs), LANES), 2 * n_pairs)
        lanes = pl.ds(chunk * width, width)

        def body(tile, _):
            rows = pl.ds(pl.multiple_of(tile * m_tile, m_tile), m_tile)
            product = lax.dot_general(
                ints[rows, lanes], amps[pairs, lanes], (((1,), (1,)), ((), ())), preferred_element_type=jnp.float32
            )
            part[rows, pairs] = product if first else part[rows, pairs] + product
            return 0

        lax.fori_loop(0, n_res // m_tile, body, 0)

    def res_rows(chip_step, core_step):
        return pl.ds(pl.multiple_of(peer(chip_step, core_step) * out_rows, 8), out_rows)

    def group_pairs(group):
        source = lax.rem(chip - group // 2 + n_chip, n_chip)
        return pl.ds(pl.multiple_of(source * (2 * n_pairs) + group % 2 * n_pairs, LANES), n_pairs)

    def pair_copy(group, chip_step):
        pairs = group_pairs(group)
        return pltpu.make_async_remote_copy(
            src_ref=part.at[res_rows(chip_step, 1), pairs], dst_ref=pair_in.at[chip_step, :, pairs],
            send_sem=pair_send.at[group, chip_step], recv_sem=pair_recv.at[group, chip_step],
            device_id={"col": peer(0, 1)}, device_id_type=MESH,
        )

    def chip_copy(group, chip_step):
        pairs = group_pairs(group)
        return pltpu.make_async_remote_copy(
            src_ref=part.at[res_rows(chip_step, 0), pairs], dst_ref=chip_in.at[chip_step - 1, :, pairs],
            send_sem=chip_send.at[group, chip_step - 1], recv_sem=chip_recv.at[group, chip_step - 1],
            device_id={"col": peer(chip_step, 0)}, device_id_type=MESH,
        )

    def chip_arrival(group, chip_step):
        pairs = group_pairs(group)
        sender_group = (group - 2 * chip_step) % n_col
        return pltpu.make_async_remote_copy(
            src_ref=part.at[res_rows(chip_step, 0), pairs], dst_ref=chip_in.at[chip_step - 1, :, pairs],
            send_sem=chip_send.at[sender_group, chip_step - 1], recv_sem=chip_recv.at[sender_group, chip_step - 1],
            device_id={"col": peer(chip_step, 0)}, device_id_type=MESH,
        )

    steps = list(range(1, n_chip)) + [0]

    def exchange(group):
        for chip_step in steps:
            pair_copy(group, chip_step).start()

    def pass_on(group):
        pairs = group_pairs(group)
        for chip_step in steps:
            pair_copy(group, chip_step).wait_recv()
            rows = res_rows(chip_step, 0)
            part[rows, pairs] = part[rows, pairs] + pair_in[chip_step, :, pairs]
            if chip_step:
                chip_copy(group, chip_step).start()

    for chunk in range(CHUNKS):
        amp_copy(0, 1, chunk).wait_recv()
        multiply(0, chunk, chunk == 0)
    exchange(0)
    exchange(1)
    for chip_step in range(1, n_chip):
        for chunk in range(CHUNKS):
            for core_step in range(2):
                amp_copy(chip_step, core_step, chunk).wait_recv()
            multiply(chip_step, chunk, chunk == 0)
            if chip_step == 1 and chunk == 0:
                pass_on(0)
                pass_on(1)
        exchange(2 * chip_step)
        exchange(2 * chip_step + 1)
    for group in range(2, n_col):
        pass_on(group)
    for group in range(n_col):
        pairs = group_pairs(group)
        total = part[res_rows(0, 0), pairs]
        for chip_step in range(1, n_chip):
            chip_arrival(group, chip_step).wait_recv()
            total = total + chip_in[chip_step - 1, :, pairs]
        out_ref[:, pairs] = total.astype(out_ref.dtype)

    for chip_step, core_step, chunk in sends:
        amp_copy(chip_step, core_step, chunk).wait_send()
    for step in range(1, n_row // 2 + 1):
        for direction, part_index in ring_moves(step):
            ring_copy(direction, step, part_index).wait_send()
    for group in range(n_col):
        for chip_step in steps:
            pair_copy(group, chip_step).wait_send()
            if chip_step:
                chip_copy(group, chip_step).wait_send()


def local(n_row, n_col, amplitudes, amp_tiles, integrals, int_tiles):
    n_pairs = amplitudes.shape[0]
    own_rows, depth = integrals.shape
    n_res, row_pairs = own_rows * n_row, n_pairs * n_col
    out_rows, n_chip = n_res // n_col, n_col // 2
    slots = n_col * CHUNKS
    return pl.pallas_call(
        functools.partial(kernel, n_row, n_col),
        out_shape=jax.ShapeDtypeStruct((out_rows, row_pairs), jnp.bfloat16),
        in_specs=[
            pl.BlockSpec(memory_space=pltpu.HBM),
            pl.BlockSpec(memory_space=pltpu.HBM),
            pl.BlockSpec(memory_space=pltpu.HBM),
            pl.BlockSpec(memory_space=pltpu.HBM),
        ],
        out_specs=pl.BlockSpec(memory_space=pltpu.VMEM),
        scratch_shapes=[
            pltpu.SMEM(amp_tiles.shape, jnp.int32),
            pltpu.SMEM(int_tiles.shape, jnp.int32),
            pltpu.SemaphoreType.DMA((2,)),
            pltpu.VMEM((slots, n_pairs, depth // CHUNKS), jnp.bfloat16),
            pltpu.VMEM((row_pairs, depth), jnp.bfloat16),
            pltpu.VMEM((own_rows, depth), jnp.bfloat16),
            pltpu.VMEM((n_res, depth), jnp.bfloat16),
            pltpu.VMEM((n_res, row_pairs), jnp.float32),
            pltpu.VMEM((n_chip, out_rows, row_pairs), jnp.float32),
            pltpu.VMEM((n_chip - 1, out_rows, row_pairs), jnp.float32),
            pltpu.SemaphoreType.DMA((slots,)),
            pltpu.SemaphoreType.DMA,
            pltpu.SemaphoreType.DMA((slots,)),
            pltpu.SemaphoreType.DMA((slots,)),
            pltpu.SemaphoreType.DMA((2, n_row // 2, 2)),
            pltpu.SemaphoreType.DMA((2, n_row // 2, 2)),
            pltpu.SemaphoreType.DMA((n_col, n_chip)),
            pltpu.SemaphoreType.DMA((n_col, n_chip)),
            pltpu.SemaphoreType.DMA((n_col, n_chip - 1)),
            pltpu.SemaphoreType.DMA((n_col, n_chip - 1)),
        ],
        compiler_params=pltpu.CompilerParams(
            collective_id=0, has_side_effects=True, vmem_limit_bytes=64 * 1024 * 1024
        ),
    )(amplitudes, amp_tiles, integrals, int_tiles)


def solution(mesh):
    return jax.shard_map(
        functools.partial(local, mesh.shape["row"], mesh.shape["col"]),
        mesh=mesh,
        in_specs=(
            P(("row", "col"), None),
            P(("row", "col"), None),
            P("row", "col"),
            P(None, "col"),
        ),
        out_specs=P("col", "row"),
        check_vma=False,
    )
```
